256 devices in a mesh: rep: 8 (over z_lo, core), fsdp: 32 (over y, z_hi, x).
Axes of the slice: x: 4, y: 4, z: 8 (z_hi: 2, z_lo: 4; z = z_hi * 4 + z_lo), core: 2. Of those that a mesh axis runs over, the one named last changes fastest.
Arguments:
- activations: bfloat16 [131072, 4096], P(('rep', 'fsdp')), may hold values from -6 to 6
- weights: bfloat16 [8, 4096, 1024], P('rep', 'fsdp'), may hold values from -0.09375 to 0.09375
- cotangent: bfloat16 [131072, 1024], P(('rep', 'fsdp')), may hold values from -6 to 6
- quant_codes: bfloat16 [8, 512, 8192], P('rep', 'fsdp'), may hold values from -6 to 6
- replica_scale: float32 [8], P('rep'), may hold values from 0.25 to 4
- outer_params: float32 [512, 8192], P('fsdp'), may hold values from -6 to 6
- momentum: float32 [512, 8192], P('fsdp'), may hold values from -4 to 4
Outputs:
- projected: bfloat16 [131072, 1024], P(('rep', 'fsdp'))
- input_grad: bfloat16 [131072, 4096], P(('rep', 'fsdp'))
- weight_grad: float32 [8, 4096, 1024], P('rep', 'fsdp')
- new_params: float32 [512, 8192], P('fsdp')
- new_momentum: float32 [512, 8192], P('fsdp')
The draws below stay inside these ranges and needn't reach their ends.
All inputs are finite; a program needn't handle non-finite values.
Results may differ from the reference program's by a relative error of at most 0.001.
Values may be sent and summed in bfloat16 or wider, within the bound.
No kernel may reach another device: no remote copies, remote signals or barrier semaphores. Data moves between devices by JAX's collectives and lax.ppermute only.
A program may use at most 128 MiB of HBM per device.

```python
import math
import jax
import jax.numpy as jnp
from jax import lax

D = 4096
KV = 1024
FW = 8192
REP_TOKENS = 16384
TOKENS = 131072
FRAG_ROWS = 512
N_REP = 8


def shard_levels(key, extent, split, least, top_value):
    level = 1.0
    for dim, parts in split:
        draws = jax.random.uniform(jax.random.fold_in(jax.random.fold_in(key, 6), dim), (parts,), jnp.float32, least / len(split), top_value / len(split))
        level = level * jnp.repeat(jnp.exp(draws), extent[dim] // parts).reshape((-1,) + (1,) * (len(extent) - 1 - dim))
    return level


def centred(key, extent, deviation, reach, split=(), kind=jnp.bfloat16):
    array = deviation * jax.random.normal(key, extent, jnp.float32)
    if split:
        array = array * shard_levels(key, extent, split, -0.22, 0.18)
    return jnp.clip(array, -reach, reach).astype(kind)


def setup_inputs(seed: int = 0) -> dict:
    streams_of = jax.random.split(jax.random.key(seed), 8)
    return {
        "activations": centred(streams_of[0], (TOKENS, D), 1.0, 6.0, ((0, 256),)),
        "weights": centred(streams_of[1], (N_REP, D, KV), D ** -0.5, 0.09375, ((0, 8), (1, 32))),
        "cotangent": centred(streams_of[2], (TOKENS, KV), 1.0, 6.0, ((0, 256),)),
        "quant_codes": centred(streams_of[3], (N_REP, FRAG_ROWS, FW), 1.0, 6.0, ((0, 8), (1, 32))),
        "replica_scale": jnp.clip(jnp.exp(math.log(4.0) - 2.7725887 * jax.random.uniform(streams_of[4], (N_REP,), jnp.float32) ** shard_levels(streams_of[4], (N_REP,), ((0, 8),), -0.2, 0.2)), 0.25, 4.0),
        "outer_params": centred(streams_of[5], (FRAG_ROWS, FW), 1.0, 6.0, ((0, 32),), jnp.float32),
        "momentum": centred(streams_of[6], (FRAG_ROWS, FW), 0.5, 4.0, ((0, 32),), jnp.float32),
    }


def reference(activations, weights, cotangent, quant_codes, replica_scale, outer_params, momentum):
    acts_rep = activations.reshape(N_REP, REP_TOKENS, D)
    cot_rep = cotangent.reshape(N_REP, REP_TOKENS, KV)
    factor = 1.0 / jnp.sqrt(jnp.float32(REP_TOKENS))

    def one_replica(inputs):
        inputs_x, weight_r, inputs_g = inputs
        forward = jnp.dot(inputs_x, weight_r, preferred_element_type=jnp.float32).astype(jnp.bfloat16)
        backward = jnp.dot(inputs_g, weight_r.T, preferred_element_type=jnp.float32).astype(jnp.bfloat16)
        gradient = jnp.dot(inputs_x.T, inputs_g, preferred_element_type=jnp.float32) * factor
        return (forward, backward, gradient)
    forward, backward, gradient = lax.map(one_replica, (acts_rep, weights, cot_rep))
    terms = replica_scale.astype(jnp.float32)[:, None, None] * quant_codes.astype(jnp.float32)
    average = lax.optimization_barrier(jnp.sum(terms, axis=0)) / N_REP
    new_momentum = 0.9 * momentum + average
    new_params = outer_params - 0.7 * (average + 0.9 * new_momentum)
    return (forward.reshape(TOKENS, KV), backward.reshape(TOKENS, D), gradient, new_params, new_momentum)
```

```python
import jax
import jax.numpy as jnp
from jax import lax
from jax.experimental import pallas as pl
from jax.experimental.pallas import tpu as pltpu
from jax.sharding import PartitionSpec as P

NX, NY, NZ = 4, 4, 2
F32, F16, BF16 = jnp.float32, jnp.float16, jnp.bfloat16


def place():
    i = lax.axis_index("fsdp")
    return i % NX, i // (NX * NZ), (i // NX) % NZ


def move(a, dx=0, dy=0, dz=0):
    pairs = []
    for y in range(NY):
        for z in range(NZ):
            for x in range(NX):
                to = (((y + dy) % NY) * NZ + (z + dz) % NZ) * NX + (x + dx) % NX
                pairs.append(((y * NZ + z) * NX + x, to))
    return lax.ppermute(a, "fsdp", pairs)


def on(axis, a, step):
    return move(a, **{"d" + axis: step})


def sort_kernel(act, cot, out, top):
    x, y, z = place()

    @pl.when(pl.program_id(0) == 0)
    def _():
        top[...] = jnp.zeros_like(top)

    for p in range(NZ):
        for jx in range(NX):
            for jy in range(NY):
                block = (((y - jy) & 3) * NZ + (z ^ p)) * NX + ((x - jx) & 3)
                lanes = pl.ds(pl.multiple_of(block * 128, 128), 128)
                out[p, jx, :, jy * 128 : (jy + 1) * 128] = act[:, lanes]

    def fold(ref):
        m = None
        for c in range(ref.shape[1] // 128):
            v = jnp.abs(ref[:, c * 128 : (c + 1) * 128].astype(F32))
            m = v if m is None else jnp.maximum(m, v)
        return jnp.max(m.reshape(-1, 8, 128), axis=0)

    top[0] = jnp.maximum(top[0], fold(act))
    top[1] = jnp.maximum(top[1], fold(cot))


def sort(act, cot):
    rows = 64
    return pl.pallas_call(
        sort_kernel,
        grid=(act.shape[0] // rows,),
        in_specs=[
            pl.BlockSpec((rows, act.shape[1]), lambda i: (i, 0)),
            pl.BlockSpec((rows, cot.shape[1]), lambda i: (i, 0)),
        ],
        out_specs=[
            pl.BlockSpec((NZ, NX, rows, 512), lambda i: (0, 0, i, 0)),
            pl.BlockSpec((2, 8, 128), lambda i: (0, 0, 0)),
        ],
        out_shape=[
            jax.ShapeDtypeStruct((NZ, NX, act.shape[0], 512), BF16),
            jax.ShapeDtypeStruct((2, 8, 128), F32),
        ],
        compiler_params=pltpu.CompilerParams(vmem_limit_bytes=16 << 20),
        cost_estimate=pl.CostEstimate(flops=0, bytes_accessed=9 << 20, transcendentals=0),
    )(act, cot)


def plane_kernel(p, last, *refs):
    n_in = 10 + (2 if last else 0)
    act, cot = refs[0], refs[1]
    pieces = refs[2:10]
    partial = refs[10] if last else None
    proj, grad = refs[n_in], refs[n_in + 1]
    act_s, cot_s, w_s, acc_s, grad_s, a_sem, w_sem, c_sem, o_sem, p_sem = refs[n_in + 2 :]
    x, y, z = place()

    def columns(j):
        group = ((y - j) & 3) * NZ + (z ^ p)
        return pl.ds(pl.multiple_of(group * 512, 512), 512)

    cot_in = pltpu.make_async_copy(cot, cot_s, c_sem)
    cot_in.start()
    for j in range(NY):
        pltpu.make_async_copy(pieces[2 * j], w_s.at[j, pl.ds(0, 256)], w_sem.at[j]).start()
        pltpu.make_async_copy(pieces[2 * j + 1], w_s.at[j, pl.ds(256, 256)], w_sem.at[j]).start()
        pltpu.make_async_copy(act.at[:, columns(j)], act_s.at[j], a_sem.at[j]).start()
    if last:
        before = pltpu.make_async_copy(partial, acc_s, p_sem)
        before.start()
        before.wait()
    else:
        acc_s[...] = jnp.zeros_like(acc_s)
    cot_in.wait()

    @pl.loop(0, NY)
    def _(j):
        pltpu.make_async_copy(w_s.at[j], w_s.at[j], w_sem.at[j]).wait()
        pltpu.make_async_copy(act_s.at[j], act_s.at[j], a_sem.at[j]).wait()
        w = jnp.concatenate(
            [w_s[j, pl.ds(pl.multiple_of(((x - xx) & 3) * 128, 128), 128), :] for xx in range(NX)], axis=0
        )
        acc_s[...] += jnp.dot(act_s[j], w, preferred_element_type=F32)
        grad_s[j] = lax.dot_general(
            cot_s[...], w, (((1,), (1,)), ((), ())), preferred_element_type=F32
        ).astype(BF16)
        pltpu.make_async_copy(grad_s.at[j], grad.at[:, columns(j)], o_sem.at[j]).start()

    proj[...] = acc_s[...].astype(proj.dtype)
    for j in range(NY):
        pltpu.make_async_copy(grad_s.at[j], grad_s.at[j], o_sem.at[j]).wait()


def plane(p, act, cot, pieces, before):
    last = before is not None
    tokens, depth = act.shape
    width = cot.shape[1]
    any_ = pl.BlockSpec(memory_space=pl.ANY)
    args = [act, cot, *pieces] + (list(before) if last else [])
    return pl.pallas_call(
        lambda *refs: plane_kernel(p, last, *refs),
        in_specs=[any_] * len(args),
        out_specs=[pl.BlockSpec(memory_space=pltpu.VMEM), any_],
        out_shape=[
            jax.ShapeDtypeStruct((tokens, width), BF16 if last else F32),
            jax.ShapeDtypeStruct((tokens, depth), BF16),
        ],
        input_output_aliases={11: 1} if last else {},
        scratch_shapes=[
            pltpu.VMEM((NY, tokens, 512), BF16),
            pltpu.VMEM((tokens, width), BF16),
            pltpu.VMEM((NY, 512, width), BF16),
            pltpu.VMEM((tokens, width), F32),
            pltpu.VMEM((NY, tokens, 512), BF16),
            pltpu.SemaphoreType.DMA((NY,)),
            pltpu.SemaphoreType.DMA((NY,)),
            pltpu.SemaphoreType.DMA,
            pltpu.SemaphoreType.DMA((NY,)),
            pltpu.SemaphoreType.DMA,
        ],
        compiler_params=pltpu.CompilerParams(vmem_limit_bytes=28 << 20),
        cost_estimate=pl.CostEstimate(flops=4 * tokens * 2048 * width, bytes_accessed=12 << 20, transcendentals=0),
    )(*args)


def gather_ring(axis, low, high):
    f_low = on(axis, low, 1)
    b_high = on(axis, high, -1)
    f_high = on(axis, high, 1)
    b_low = on(axis, low, -1)
    o_low = on(axis, f_low, 1)
    o_high = on(axis, b_high, -1)
    return [(low, high), (f_low, f_high), (o_low, o_high), (b_low, b_high)]


def reduce_ring(axis, slots):
    up, far, down = slots[3], slots[2], slots[1]
    f_far = on(axis, far[0], 1)
    b_far = on(axis, far[1], -1)
    f_high = on(axis, up[1], 1)
    b_low = on(axis, down[0], -1)
    f_low = on(axis, (up[0].astype(F32) + f_far.astype(F32)).astype(F16), 1)
    b_high = on(axis, (down[1].astype(F32) + b_far.astype(F32)).astype(F16), -1)
    low = slots[0][0].astype(F32) + b_low.astype(F32) + f_low.astype(F32)
    high = slots[0][1].astype(F32) + f_high.astype(F32) + b_high.astype(F32)
    return low, high


def gather_plane(chunk):
    half = chunk.shape[0] // 2
    w = gather_ring("x", chunk[:half], chunk[half:])
    first = jnp.concatenate([chunk, *w[1]], axis=0)
    second = jnp.concatenate([*w[2], *w[3]], axis=0)
    return [piece for pair in gather_ring("y", first, second) for piece in pair]


def reduce_plane(act_sorted, cot, scale):
    half = cot.shape[1] // 2

    def term(j, c):
        g = jnp.einsum("td,tk->dk", act_sorted[j], c, preferred_element_type=F32)
        return (g * scale).astype(F16)

    slots = {j: (term(j, cot[:, :half]), term(j, cot[:, half:])) for j in (2, 3, 1, 0)}
    low, high = reduce_ring("x", slots)
    low, high = low.astype(F16), high.astype(F16)
    rows = low.shape[0] // NY
    slots = [(low[j * rows : (j + 1) * rows], high[j * rows : (j + 1) * rows]) for j in range(NY)]
    return jnp.concatenate(reduce_ring("y", slots), axis=1)


def sum_of_replicas(codes, scale):
    i = lax.axis_index("rep")
    n = lax.axis_size("rep")
    core = i % 2
    half = codes.shape[1] // 2

    def swap(a, bit):
        return lax.ppermute(a, "rep", [(j, j ^ bit) for j in range(n)])

    keep = lax.dynamic_slice(codes, (0, core * half), (codes.shape[0], half)).astype(F32) * scale
    give = lax.dynamic_slice(codes, (0, (1 - core) * half), (codes.shape[0], half)).astype(F32) * scale
    total = keep + swap(give, 1)
    total = total + swap(total, 2)
    total = total + swap(total, 4)
    other = swap(total, 1)
    return jnp.where(core == 0, jnp.concatenate([total, other], 1), jnp.concatenate([other, total], 1))


def common_scale(top, tokens):
    for axis in ("x", "y"):
        parts = [on(axis, top, s) for s in (1, -1, 2)]
        top = jnp.maximum(jnp.maximum(top, parts[0]), jnp.maximum(parts[1], parts[2]))
    top = jnp.maximum(top, move(top, dz=1))
    bound = jnp.max(top[0]) * jnp.max(top[1]) * tokens
    bound = jnp.maximum(bound, 1e-30)
    return 32768.0 / bound, bound / 32768.0


def outer_step(average, params_rows, moment_rows):
    moment_next = 0.9 * moment_rows + average
    params_next = params_rows - 0.7 * (average + 0.9 * moment_next)
    return params_next, moment_next


def local(activations, weights, cotangent, quant_codes, replica_scale, outer_params, momentum):
    chunk = weights[0]
    far_chunk = move(chunk, dz=1)
    near = gather_plane(chunk)
    far = gather_plane(far_chunk)

    replica_tokens = activations.shape[0] * lax.axis_size("fsdp")
    act_sorted, top = sort(activations, cotangent)
    scale, unscale = common_scale(top, replica_tokens)
    theirs = reduce_plane(act_sorted[1], cotangent, scale).astype(F16)
    mine = reduce_plane(act_sorted[0], cotangent, scale)
    total = mine + move(theirs, dz=1).astype(F32)
    gradient = total * (unscale * (1.0 / jnp.sqrt(jnp.float32(replica_tokens))))

    part = plane(0, activations, cotangent, near, None)
    projected, input_grad = plane(1, activations, cotangent, far, part)

    average = sum_of_replicas(quant_codes[0], replica_scale[0]) / lax.axis_size("rep")
    new_params, new_momentum = outer_step(average, outer_params, momentum)
    return projected, input_grad, gradient[None], new_params, new_momentum


def solution(mesh):
    placed = (
        P(("rep", "fsdp"), None),
        P("rep", "fsdp", None),
        P(("rep", "fsdp"), None),
        P("rep", "fsdp", None),
        P("rep"),
        P("fsdp", None),
        P("fsdp", None),
    )
    return jax.shard_map(
        local,
        mesh=mesh,
        in_specs=placed,
        out_specs=(
            P(("rep", "fsdp"), None),
            P(("rep", "fsdp"), None),
            P("rep", "fsdp", None),
            P("fsdp", None),
            P("fsdp", None),
        ),
        check_vma=False,
    )
```

```python
import jax
import jax.numpy as jnp
from jax import lax
from jax.experimental import pallas as pl
from jax.experimental.pallas import tpu as pltpu
from jax.sharding import PartitionSpec as P

NX, NY, NZ = 4, 4, 2
F32, F16, BF16 = jnp.float32, jnp.float16, jnp.bfloat16


def place():
    i = lax.axis_index("fsdp")
    return i % NX, i // (NX * NZ), (i // NX) % NZ


def move(a, dx=0, dy=0, dz=0):
    pairs = []
    for y in range(NY):
        for z in range(NZ):
            for x in range(NX):
                to = (((y + dy) % NY) * NZ + (z + dz) % NZ) * NX + (x + dx) % NX
                pairs.append(((y * NZ + z) * NX + x, to))
    return lax.ppermute(a, "fsdp", pairs)


def on(axis, a, step):
    return move(a, **{"d" + axis: step})


BUFFERS = (
    ((2, 0), (2, 1), (3, 2), (3, 3)),
    ((2, 2), (2, 3), (1, 0), (1, 1)),
    ((3, 0), (3, 1), (1, 2), (1, 3)),
    ((0, 0), (0, 1), (0, 2), (0, 3)),
)


def sort_kernel(act, cot, out, top):
    x, y, z = place()

    @pl.when(pl.program_id(0) == 0)
    def _():
        top[...] = jnp.zeros_like(top)

    for p in range(NZ):
        for b, slots in enumerate(BUFFERS):
            for k, (jx, jy) in enumerate(slots):
                block = (((y - jy) & 3) * NZ + (z ^ p)) * NX + ((x - jx) & 3)
                lanes = pl.ds(pl.multiple_of(block * 128, 128), 128)
                out[p, b, :, k * 128 : (k + 1) * 128] = act[:, lanes]

    def fold(ref):
        m = None
        for c in range(ref.shape[1] // 128):
            v = jnp.abs(ref[:, c * 128 : (c + 1) * 128].astype(F32))
            m = v if m is None else jnp.maximum(m, v)
        return jnp.max(m.reshape(-1, 8, 128), axis=0)

    top[0] = jnp.maximum(top[0], fold(act))
    top[1] = jnp.maximum(top[1], fold(cot))


def sort(act, cot):
    rows = 64
    return pl.pallas_call(
        sort_kernel,
        grid=(act.shape[0] // rows,),
        in_specs=[
            pl.BlockSpec((rows, act.shape[1]), lambda i: (i, 0)),
            pl.BlockSpec((rows, cot.shape[1]), lambda i: (i, 0)),
        ],
        out_specs=[
            pl.BlockSpec((NZ, NX, rows, 512), lambda i: (0, 0, i, 0)),
            pl.BlockSpec((2, 8, 128), lambda i: (0, 0, 0)),
        ],
        out_shape=[
            jax.ShapeDtypeStruct((NZ, NX, act.shape[0], 512), BF16),
            jax.ShapeDtypeStruct((2, 8, 128), F32),
        ],
        compiler_params=pltpu.CompilerParams(vmem_limit_bytes=16 << 20),
        cost_estimate=pl.CostEstimate(flops=0, bytes_accessed=9 << 20, transcendentals=0),
    )(act, cot)


def plane_kernel(p, last, *refs):
    n_in = 7 + (2 if last else 0)
    act, cot = refs[0], refs[1]
    pieces = refs[2:7]
    partial = refs[7] if last else None
    proj, grad = refs[n_in], refs[n_in + 1]
    act_s, cot_s, w_s, acc_s, grad_s, a_sem, w_sem, c_sem, o_sem, p_sem = refs[n_in + 2 :]
    x, y, z = place()

    def columns(j):
        group = ((y - j) & 3) * NZ + (z ^ p)
        return pl.ds(pl.multiple_of(group * 512, 512), 512)

    cot_in = pltpu.make_async_copy(cot, cot_s, c_sem)
    cot_in.start()
    own, below, far_low, far_high, above = pieces
    parts = {0: [own], 1: [below], 2: [far_low, far_high], 3: [above]}
    for j in range(NY):
        row = 0
        for part in parts[j]:
            to = w_s.at[j, pl.ds(row, part.shape[0])]
            pltpu.make_async_copy(part, to, w_sem.at[j]).start()
            row += part.shape[0]
        pltpu.make_async_copy(act.at[:, columns(j)], act_s.at[j], a_sem.at[j]).start()
    if last:
        before = pltpu.make_async_copy(partial, acc_s, p_sem)
        before.start()
        before.wait()
    else:
        acc_s[...] = jnp.zeros_like(acc_s)
    cot_in.wait()

    @pl.loop(0, NY)
    def _(j):
        pltpu.make_async_copy(w_s.at[j], w_s.at[j], w_sem.at[j]).wait()
        pltpu.make_async_copy(act_s.at[j], act_s.at[j], a_sem.at[j]).wait()
        w = jnp.concatenate(
            [w_s[j, pl.ds(pl.multiple_of(((x - xx) & 3) * 128, 128), 128), :] for xx in range(NX)], axis=0
        )
        acc_s[...] += jnp.dot(act_s[j], w, preferred_element_type=F32)
        grad_s[j] = lax.dot_general(
            cot_s[...], w, (((1,), (1,)), ((), ())), preferred_element_type=F32
        ).astype(BF16)
        pltpu.make_async_copy(grad_s.at[j], grad.at[:, columns(j)], o_sem.at[j]).start()

    proj[...] = acc_s[...].astype(proj.dtype)
    for j in range(NY):
        pltpu.make_async_copy(grad_s.at[j], grad_s.at[j], o_sem.at[j]).wait()


def plane(p, act, cot, pieces, before):
    last = before is not None
    tokens, depth = act.shape
    width = cot.shape[1]
    any_ = pl.BlockSpec(memory_space=pl.ANY)
    args = [act, cot, *pieces] + (list(before) if last else [])
    return pl.pallas_call(
        lambda *refs: plane_kernel(p, last, *refs),
        in_specs=[any_] * len(args),
        out_specs=[pl.BlockSpec(memory_space=pltpu.VMEM), any_],
        out_shape=[
            jax.ShapeDtypeStruct((tokens, width), BF16 if last else F32),
            jax.ShapeDtypeStruct((tokens, depth), BF16),
        ],
        input_output_aliases={8: 1} if last else {},
        scratch_shapes=[
            pltpu.VMEM((NY, tokens, 512), BF16),
            pltpu.VMEM((tokens, width), BF16),
            pltpu.VMEM((NY, 512, width), BF16),
            pltpu.VMEM((tokens, width), F32),
            pltpu.VMEM((NY, tokens, 512), BF16),
            pltpu.SemaphoreType.DMA((NY,)),
            pltpu.SemaphoreType.DMA((NY,)),
            pltpu.SemaphoreType.DMA,
            pltpu.SemaphoreType.DMA((NY,)),
            pltpu.SemaphoreType.DMA,
        ],
        compiler_params=pltpu.CompilerParams(vmem_limit_bytes=28 << 20),
        cost_estimate=pl.CostEstimate(flops=4 * tokens * 2048 * width, bytes_accessed=12 << 20, transcendentals=0),
    )(*args)


class Lanes:
    def __init__(self):
        self.last = {}

    def send(self, lane, a, **step):
        if lane in self.last:
            a, _ = lax.optimization_barrier((a, self.last[lane]))
        r = move(a, **step)
        self.last[lane] = r
        return r

    def both(self, axis, forward, backward):
        f = self.send(axis + "+", forward, **{"d" + axis: 1})
        b = self.send(axis + "-", backward, **{"d" + axis: -1})
        return f, b


def gather_ring(lanes, axis, a):
    half = a.shape[0] // 2
    f, b = lanes.both(axis, a, a)
    low, high = lanes.both(axis, f[:half], b[half:])
    return [a, f, low, high, b]


def wide(*parts):
    total = parts[0].astype(F32)
    for p in parts[1:]:
        total = total + p.astype(F32)
    return total


def reduce_x(lanes, buffers):
    half = buffers[0].shape[0] // 2
    f, b = lanes.both("x", buffers[0], buffers[1])
    up = wide(buffers[2][:half], f[:half]).astype(F16)
    down = wide(buffers[2][half:], b[:half]).astype(F16)
    f2, b2 = lanes.both("x", up, down)
    low = wide(buffers[3][:half], b[half:], f2).astype(F16)
    high = wide(buffers[3][half:], f[half:], b2).astype(F16)
    return jnp.concatenate([low, high], axis=0)


def reduce_y(lanes, a):
    n = a.shape[0] // NY
    h = n // 2
    f, b = lanes.both("y", a[2 * n + h : 3 * n + h], a[n + h : 2 * n + h])
    up = wide(a[3 * n + h :], f[:h]).astype(F16)
    down = wide(a[n : n + h], b[h:]).astype(F16)
    f2, b2 = lanes.both("y", up, down)
    return jnp.concatenate([wide(a[:h], f[h:], b2), wide(a[h:n], b[:h], f2)], axis=0)


def gather_x(lanes, chunk):
    return jnp.concatenate(gather_ring(lanes, "x", chunk), axis=0)


def terms(act_sorted, cot, scale):
    out = []
    for b in range(len(BUFFERS)):
        g = jnp.einsum("td,tk->dk", act_sorted[b], cot, preferred_element_type=F32)
        out.append((g * scale).astype(F16))
    return out


def sum_of_replicas(lanes, codes, scale):
    i = lax.axis_index("rep")
    n = lax.axis_size("rep")
    core = i % 2
    half = codes.shape[1] // 2

    def swap(a, bit):
        a, _ = lax.optimization_barrier((a, lanes.last["z"]))
        r = lax.ppermute(a, "rep", [(j, j ^ bit) for j in range(n)])
        lanes.last["z"] = r
        return r

    keep = lax.dynamic_slice(codes, (0, core * half), (codes.shape[0], half)).astype(F32) * scale
    give = lax.dynamic_slice(codes, (0, (1 - core) * half), (codes.shape[0], half)).astype(F32) * scale
    total = keep + swap(give, 1)
    total = total + swap(total, 2)
    total = total + swap(total, 4)
    other = swap(total, 1)
    return jnp.where(core == 0, jnp.concatenate([total, other], 1), jnp.concatenate([other, total], 1))


def common_scale(top, tokens):
    for axis in ("x", "y"):
        parts = [on(axis, top, s) for s in (1, -1, 2)]
        top = jnp.maximum(jnp.maximum(top, parts[0]), jnp.maximum(parts[1], parts[2]))
    top = jnp.maximum(top, move(top, dz=1))
    bound = jnp.max(top[0]) * jnp.max(top[1]) * tokens
    bound = jnp.maximum(bound, 1e-30)
    return 32768.0 / bound, bound / 32768.0


def outer_step(average, params_rows, moment_rows):
    moment_next = 0.9 * moment_rows + average
    params_next = params_rows - 0.7 * (average + 0.9 * moment_next)
    return params_next, moment_next


def local(activations, weights, cotangent, quant_codes, replica_scale, outer_params, momentum):
    chunk = weights[0]
    lanes = Lanes()
    far_chunk = lanes.send("z", chunk, dz=1)
    near_row = gather_x(lanes, chunk)

    replica_tokens = activations.shape[0] * lax.axis_size("fsdp")
    act_sorted, top = sort(activations, cotangent)
    scale, unscale = common_scale(top, replica_tokens)

    near = gather_ring(lanes, "y", near_row)
    far_row = gather_x(lanes, far_chunk)
    far = gather_ring(lanes, "y", far_row)
    theirs = reduce_x(lanes, terms(act_sorted[1], cotangent, scale))
    mine = reduce_x(lanes, terms(act_sorted[0], cotangent, scale))
    average = sum_of_replicas(lanes, quant_codes[0], replica_scale[0]) / lax.axis_size("rep")
    theirs = reduce_y(lanes, theirs).astype(F16)
    theirs = lanes.send("z", theirs, dz=1)
    mine = reduce_y(lanes, mine)
    total = mine + theirs.astype(F32)
    gradient = total * (unscale * (1.0 / jnp.sqrt(jnp.float32(replica_tokens))))

    part = plane(0, activations, cotangent, near, None)
    projected, input_grad = plane(1, activations, cotangent, far, part)

    new_params, new_momentum = outer_step(average, outer_params, momentum)
    return projected, input_grad, gradient[None], new_params, new_momentum


def solution(mesh):
    placed = (
        P(("rep", "fsdp"), None),
        P("rep", "fsdp", None),
        P(("rep", "fsdp"), None),
        P("rep", "fsdp", None),
        P("rep"),
        P("fsdp", None),
        P("fsdp", None),
    )
    return jax.shard_map(
        local,
        mesh=mesh,
        in_specs=placed,
        out_specs=(
            P(("rep", "fsdp"), None),
            P(("rep", "fsdp"), None),
            P("rep", "fsdp", None),
            P("fsdp", None),
            P("fsdp", None),
        ),
        check_vma=False,
    )
```

```python
import jax
import jax.numpy as jnp
from jax import lax
from jax.experimental import pallas as pl
from jax.experimental.pallas import tpu as pltpu
from jax.sharding import PartitionSpec as P

NX, NY, NZ, NR = 4, 4, 2, 8
NOTE = 16
LOW = 512
F32, F16, BF16 = jnp.float32, jnp.float16, jnp.bfloat16


def place():
    i = lax.axis_index("fsdp")
    x, y, z = i % NX, i // (NX * NZ), (i // NX) % NZ
    turned = lax.axis_index("rep") % 2
    return x + turned * (y - x), y + turned * (x - y), z, turned


def feature_block(u, v, z, turned):
    x, y = u + turned * (v - u), v + turned * (u - v)
    return (y * NZ + z) * NX + x


def move(a, change):
    pairs = []
    for r in range(NR):
        for y in range(NY):
            for z in range(NZ):
                for x in range(NX):
                    u, v, w = change(*((y, x) if r % 2 else (x, y)), z)
                    to_x, to_y = (v, u) if r % 2 else (u, v)
                    here = (y * NZ + z) * NX + x
                    there = ((to_y % NY) * NZ + w % NZ) * NX + to_x % NX
                    pairs.append((r * NX * NY * NZ + here, r * NX * NY * NZ + there))
    return lax.ppermute(a, ("rep", "fsdp"), pairs)


STEPS = {
    "u+": lambda u, v, z: (u + 1, v, z),
    "u-": lambda u, v, z: (u - 1, v, z),
    "v+": lambda u, v, z: (u, v + 1, z),
    "v-": lambda u, v, z: (u, v - 1, z),
    "z": lambda u, v, z: (u, v, z + 1),
    "uu": lambda u, v, z: (u + 2, v, z),
    "vv": lambda u, v, z: (u, v + 2, z),
}


def after(a, *others):
    return lax.optimization_barrier((a, others))[0]


BUFFERS = (
    ((2, 0), (2, 1), (3, 2), (3, 3)),
    ((2, 2), (2, 3), (1, 0), (1, 1)),
    ((3, 0), (3, 1), (1, 2), (1, 3)),
    ((0, 0), (0, 1), (0, 2), (0, 3)),
)


CHUNK = 64


def sort_kernel(act, cot, out, top, act_s, cot_s, out_s, in_sem, out_sem):
    u, v, z, turned = place()
    count = act.shape[0] // CHUNK
    for c in range(count):
        rows = pl.ds(c * CHUNK, CHUNK)
        pltpu.make_async_copy(act.at[rows], act_s.at[c], in_sem.at[0, c]).start()
        pltpu.make_async_copy(cot.at[rows], cot_s.at[c], in_sem.at[1, c]).start()

    def fold(value):
        m = None
        for i in range(value.shape[1] // 128):
            part = jnp.abs(value[:, i * 128 : (i + 1) * 128])
            m = part if m is None else jnp.maximum(m, part)
        return jnp.max(m.astype(F32).reshape(-1, 8, 128), axis=0)

    top[...] = jnp.zeros_like(top)

    @pl.loop(0, count)
    def _(c):
        pltpu.make_async_copy(act_s.at[c], act_s.at[c], in_sem.at[0, c]).wait()
        pltpu.make_async_copy(cot_s.at[c], cot_s.at[c], in_sem.at[1, c]).wait()
        for p in range(NZ):
            for b, slots in enumerate(BUFFERS):
                for k, (ju, jv) in enumerate(slots):
                    block = feature_block((u - ju) & 3, (v - jv) & 3, z ^ p, turned)
                    lanes = pl.ds(pl.multiple_of(block * 128, 128), 128)
                    out_s[c, p, b, :, k * 128 : (k + 1) * 128] = act_s[c, :, lanes]
        top[0] = jnp.maximum(top[0], fold(act_s[c]))
        top[1] = jnp.maximum(top[1], fold(cot_s[c]))
        rows = pl.ds(pl.multiple_of(c * CHUNK, CHUNK), CHUNK)
        pltpu.make_async_copy(out_s.at[c], out.at[:, :, rows], out_sem.at[c]).start()

    for c in range(count):
        pltpu.make_async_copy(out_s.at[c], out_s.at[c], out_sem.at[c]).wait()


def sort(act, cot):
    count = act.shape[0] // CHUNK
    any_ = pl.BlockSpec(memory_space=pl.ANY)
    return pl.pallas_call(
        sort_kernel,
        in_specs=[any_, any_],
        out_specs=[any_, pl.BlockSpec(memory_space=pltpu.VMEM)],
        out_shape=[
            jax.ShapeDtypeStruct((NZ, NX, act.shape[0], 512), BF16),
            jax.ShapeDtypeStruct((2, 8, 128), F32),
        ],
        scratch_shapes=[
            pltpu.VMEM((count, CHUNK, act.shape[1]), BF16),
            pltpu.VMEM((count, CHUNK, cot.shape[1]), BF16),
            pltpu.VMEM((count, NZ, NX, CHUNK, 512), BF16),
            pltpu.SemaphoreType.DMA((2, count)),
            pltpu.SemaphoreType.DMA((count,)),
        ],
        compiler_params=pltpu.CompilerParams(vmem_limit_bytes=56 << 20),
        cost_estimate=pl.CostEstimate(flops=0, bytes_accessed=1 << 20, transcendentals=0),
    )(act, cot)


def product_kernel(counts, before, *refs):
    act, cot = refs[0], refs[1]
    n = 2 + sum(counts.values())
    pieces = list(refs[2:n])
    partial = refs[n] if before else None
    n += 2 if before else 0
    proj, grad = refs[n], refs[n + 1]
    act_s, cot_s, w_s, acc_s, grad_s, a_sem, w_sem, c_sem, o_sem, p_sem = refs[n + 2 :]
    u, v, z, turned = place()

    def columns(p, ju, jv):
        block = feature_block((u - ju) & 3, (v - jv) & 3, z ^ p, turned)
        return pl.ds(pl.multiple_of(block * 128, 128), 128)

    cot_in = pltpu.make_async_copy(cot, cot_s, c_sem)
    cot_in.start()
    if before:
        sums_in = pltpu.make_async_copy(partial, acc_s, p_sem)
        sums_in.start()
    units = []
    for j, count in counts.items():
        halves = []
        for _ in range(count):
            part = pieces.pop(0)
            halves += [(part, begin) for begin in (0, LOW) if begin < part.shape[0]]
        units += [(p, j, [(part, begin + p * 256) for part, begin in halves]) for p in range(NZ)]
    for k, (p, j, halves) in enumerate(units):
        for h, (part, begin) in enumerate(halves):
            to = w_s.at[k, pl.ds(h * 256, 256)]
            pltpu.make_async_copy(part.at[pl.ds(begin, 256)], to, w_sem.at[k]).start()
        for i in range(NX):
            to = act_s.at[k, :, pl.ds(i * 128, 128)]
            pltpu.make_async_copy(act.at[:, columns(p, i, j)], to, a_sem.at[k]).start()
    cot_in.wait()
    if before:
        sums_in.wait()
    for k, (p, j, _) in enumerate(units):
        pltpu.make_async_copy(w_s.at[k], w_s.at[k], w_sem.at[k]).wait()
        pltpu.make_async_copy(act_s.at[k], act_s.at[k], a_sem.at[k]).wait()
        w = w_s[k]
        term = jnp.dot(act_s[k], w, preferred_element_type=F32)
        if k == 0 and not before:
            acc_s[...] = term
        else:
            acc_s[...] += term
        grad_s[k] = lax.dot_general(
            cot_s[...], w, (((1,), (1,)), ((), ())), preferred_element_type=F32
        ).astype(BF16)
        for i in range(NX):
            out = grad_s.at[k, :, pl.ds(i * 128, 128)]
            pltpu.make_async_copy(out, grad.at[:, columns(p, i, j)], o_sem.at[k]).start()
    proj[...] = acc_s[...].astype(proj.dtype)
    for k in range(len(units)):
        pltpu.make_async_copy(grad_s.at[k], grad_s.at[k], o_sem.at[k]).wait()


def products(act, cot, pieces, before=(), last=False):
    tokens, depth = act.shape
    width = cot.shape[1]
    counts = {j: len(parts) for j, parts in pieces.items()}
    flat = [part for parts in pieces.values() for part in parts]
    n = NZ * len(pieces)
    any_ = pl.BlockSpec(memory_space=pl.ANY)
    args = [act, cot, *flat, *before]
    return pl.pallas_call(
        lambda *refs: product_kernel(counts, bool(before), *refs),
        in_specs=[any_] * len(args),
        out_specs=[pl.BlockSpec(memory_space=pltpu.VMEM), any_],
        out_shape=[
            jax.ShapeDtypeStruct((tokens, width), BF16 if last else F32),
            jax.ShapeDtypeStruct((tokens, depth), BF16),
        ],
        input_output_aliases={len(args) - 1: 1} if before else {},
        scratch_shapes=[
            pltpu.VMEM((n, tokens, 512), BF16),
            pltpu.VMEM((tokens, width), BF16),
            pltpu.VMEM((n, 512, width), BF16),
            pltpu.VMEM((tokens, width), F32),
            pltpu.VMEM((n, tokens, 512), BF16),
            pltpu.SemaphoreType.DMA((n,)),
            pltpu.SemaphoreType.DMA((n,)),
            pltpu.SemaphoreType.DMA,
            pltpu.SemaphoreType.DMA((n,)),
            pltpu.SemaphoreType.DMA,
        ],
        compiler_params=pltpu.CompilerParams(vmem_limit_bytes=(8 + 3 * n) << 20),
        cost_estimate=pl.CostEstimate(flops=0, bytes_accessed=1 << 20, transcendentals=0),
    )(*args)


class Lanes:
    def __init__(self):
        self.last = {}

    def queue(self, lane, a, shift):
        if lane in self.last:
            a = after(a, self.last[lane])
        r = shift(a)
        self.last[lane] = r
        return r

    def send(self, lane, a, step=None):
        return self.queue(lane, a, lambda a: move(a, STEPS[step or lane]))

    def both(self, axis, forward, backward, lane=""):
        up, down = axis + "+", axis + "-"
        pair = self.send(lane + up, forward, up), self.send(lane + down, backward, down)
        return lax.optimization_barrier(pair)


def gather_v(lanes, a):
    f, b = lanes.both("v", a, a)
    low, high = lanes.both("v", f[:LOW], b[LOW:])
    return [a, f, low, high, b]


def join_kernel(cuts, *refs):
    arrays, out, sem = refs[:-2], refs[-2], refs[-1]
    copies = []
    for k, (which, begin, rows) in enumerate(cuts):
        from_ = arrays[which].at[pl.ds(begin, rows)]
        copies.append(pltpu.make_async_copy(from_, out.at[pl.ds(k * rows, rows)], sem.at[k]))
    for copy in copies:
        copy.start()
    for copy in copies:
        copy.wait()


def join(arrays, cuts):
    width = arrays[0].shape[1]
    total = sum(rows for _, _, rows in cuts)
    any_ = pl.BlockSpec(memory_space=pl.ANY)
    return pl.pallas_call(
        lambda *refs: join_kernel(cuts, *refs),
        in_specs=[any_] * len(arrays),
        out_specs=any_,
        out_shape=jax.ShapeDtypeStruct((total, width), arrays[0].dtype),
        scratch_shapes=[pltpu.SemaphoreType.DMA((len(cuts),))],
        compiler_params=pltpu.CompilerParams(vmem_limit_bytes=1 << 20),
        cost_estimate=pl.CostEstimate(flops=0, bytes_accessed=1 << 20, transcendentals=0),
    )(*arrays)


def gather_u(lanes, near, far, note):
    n = near.shape[0]
    own = jnp.concatenate([near, far, note], axis=0)
    f, o, b = all_of_ring(lanes, "u", own, own, own)
    row = join((own, f, o, b), [(m, p * n, n) for pair in ((0, 1), (2, 3)) for p in range(NZ) for m in pair])
    notes = [x[2 * n :, :128].astype(F32) for x in (own, f, o, b)]
    return row, jnp.maximum(jnp.maximum(notes[0], notes[1]), jnp.maximum(notes[2], notes[3]))


def all_of_ring(lanes, axis, up, far, down, lane=""):
    f, b = lanes.both(axis, up, down, lane)
    return f, lanes.send(lane + "e", far, 2 * axis), b


def wide(*parts):
    total = parts[0].astype(F32)
    for p in parts[1:]:
        total = total + p.astype(F32)
    return total


def first_sums(buffers, arrived):
    half = buffers[0].shape[0] // 2
    f, b = arrived
    up = wide(buffers[2][:half], f[:half]).astype(F16)
    down = wide(buffers[2][half:], b[:half]).astype(F16)
    return up, down


def last_sums(buffers, arrived, sums):
    half = buffers[0].shape[0] // 2
    f, b = arrived
    f2, b2 = sums
    low = wide(buffers[3][:half], b[half:], f2)
    high = wide(buffers[3][half:], f[half:], b2)
    return [part.astype(F16) for part in (low, high)]


def with_note(a, exponent):
    note = jnp.broadcast_to(exponent.astype(F16), (NOTE, a.shape[1]))
    return jnp.concatenate([a, note], axis=0)


def exponent_in(a):
    return a[-NOTE : 1 - NOTE].astype(F32)


def reduce_v(lanes, low, high, exponent, behind, lane=""):
    n = low.shape[0] // 2
    low, high = after((low, high), *behind)
    sent = [with_note(part, exponent) for part in (high[n:], high[:n], low[n:])]
    got = all_of_ring(lanes, "v", *sent, lane)
    exponents = [exponent_in(part) for part in got]
    least = exponent
    for e in exponents:
        least = jnp.minimum(least, e)
    total = low[:n].astype(F32) * jnp.exp2(least - exponent)
    for part, e in zip(got, exponents):
        total = total + part[:-NOTE].astype(F32) * jnp.exp2(least - e)
    return total, least


def terms(act_sorted, cot, scale):
    out = []
    for part in act_sorted:
        g = jnp.einsum("td,tk->dk", part, cot, preferred_element_type=F32)
        out.append((g * scale).astype(F16))
    return out


def sum_of_replicas(lanes, codes, scale, phases):
    total = codes.astype(F32) * scale
    for bit in (1, 2, 4):
        pairs = [(j, j ^ bit) for j in range(NR)]
        if bit > 1:
            total = after(total, phases[bit // 2 - 1])
        total = total + lanes.queue("r", total, lambda a: lax.ppermute(a, "rep", pairs))
    return total


def exponent_for(note, tokens):
    bound = note[0, 0] * note[NOTE // 2, 0] * tokens
    return jnp.floor(jnp.log2(32768.0 / jnp.maximum(bound, 1e-30)))


def outer_step(average, params_rows, moment_rows):
    moment_next = 0.9 * moment_rows + average
    params_next = params_rows - 0.7 * (average + 0.9 * moment_next)
    return params_next, moment_next


def local(activations, weights, cotangent, quant_codes, replica_scale, outer_params, momentum):
    tokens = activations.shape[0] * lax.axis_size("fsdp")
    lanes = Lanes()
    shard = weights[0]
    far_shard = lanes.send("z", shard)
    act_sorted, top = sort(activations, cotangent)
    note = jnp.broadcast_to(jnp.max(top, axis=(1, 2))[:, None, None], (2, NOTE // 2, shard.shape[1]))
    row, note = gather_u(lanes, shard, far_shard, note.reshape(NOTE, -1).astype(BF16))
    exponent = exponent_for(note, tokens)
    scale = after(jnp.exp2(exponent), row)
    theirs = terms(act_sorted[1][:2], cotangent, scale)
    own, below, far_low, far_high, above = gather_v(lanes, row)
    theirs_in = lanes.both("u", theirs[0], theirs[1])
    phases = (far_shard, row)
    average = sum_of_replicas(lanes, quant_codes[0], replica_scale[0], phases) / lax.axis_size("rep")
    ready = after(cotangent, theirs, average)
    part = products(activations, ready, {0: [own]})
    theirs += terms(act_sorted[1][2:], ready, scale)
    mine = terms(act_sorted[0], cotangent, after(scale, theirs_in))

    sums = after(first_sums(theirs, theirs_in), below, above, part)
    theirs = last_sums(theirs, theirs_in, lanes.both("u", *sums))
    mine_in = lanes.both("u", *after((mine[0], mine[1]), far_low, far_high))
    theirs, their_exponent = reduce_v(lanes, *theirs, exponent, (), "theirs ")
    theirs = with_note(theirs.astype(F16), their_exponent)
    part = products(activations, after(cotangent, theirs), {1: [below], 3: [above]}, part)

    sums = after(first_sums(mine, mine_in), theirs, part)
    theirs = lanes.send("z", theirs)
    projected, input_grad = products(activations, after(cotangent, sums), {2: [far_low, far_high]}, part, last=True)
    mine = last_sums(mine, mine_in, lanes.both("u", *sums))
    mine, my_exponent = reduce_v(lanes, *mine, exponent, (projected, input_grad))
    total = mine * jnp.exp2(-my_exponent) + theirs[:-NOTE].astype(F32) * jnp.exp2(-exponent_in(theirs))
    gradient = total * (1.0 / jnp.sqrt(jnp.float32(tokens)))

    new_params, new_momentum = outer_step(average, outer_params, momentum)
    return projected, input_grad, gradient[None], new_params, new_momentum


def solution(mesh):
    placed = (
        P(("rep", "fsdp"), None),
        P("rep", "fsdp", None),
        P(("rep", "fsdp"), None),
        P("rep", "fsdp", None),
        P("rep"),
        P("fsdp", None),
        P("fsdp", None),
    )
    return jax.shard_map(
        local,
        mesh=mesh,
        in_specs=placed,
        out_specs=(
            P(("rep", "fsdp"), None),
            P(("rep", "fsdp"), None),
            P("rep", "fsdp", None),
            P("fsdp", None),
            P("fsdp", None),
        ),
        check_vma=False,
    )
```

```python
import jax
import jax.numpy as jnp
from jax import lax
from jax.experimental import pallas as pl
from jax.experimental.pallas import tpu as pltpu
from jax.sharding import PartitionSpec as P

NX, NY, NZ, NR = 4, 4, 2, 8
NOTE = 16
LOW = 512
F32, F16, BF16 = jnp.float32, jnp.float16, jnp.bfloat16


def place():
    i = lax.axis_index("fsdp")
    x, y, z = i % NX, i // (NX * NZ), (i // NX) % NZ
    turned = lax.axis_index("rep") % 2
    return x + turned * (y - x), y + turned * (x - y), z, turned


def feature_block(u, v, z, turned):
    x, y = u + turned * (v - u), v + turned * (u - v)
    return (y * NZ + z) * NX + x


def move(a, change):
    pairs = []
    for r in range(NR):
        for y in range(NY):
            for z in range(NZ):
                for x in range(NX):
                    u, v, w = change(*((y, x) if r % 2 else (x, y)), z)
                    to_x, to_y = (v, u) if r % 2 else (u, v)
                    here = (y * NZ + z) * NX + x
                    there = ((to_y % NY) * NZ + w % NZ) * NX + to_x % NX
                    pairs.append((r * NX * NY * NZ + here, r * NX * NY * NZ + there))
    return lax.ppermute(a, ("rep", "fsdp"), pairs)


STEPS = {
    "u+": lambda u, v, z: (u + 1, v, z),
    "u-": lambda u, v, z: (u - 1, v, z),
    "v+": lambda u, v, z: (u, v + 1, z),
    "v-": lambda u, v, z: (u, v - 1, z),
    "z": lambda u, v, z: (u, v, z + 1),
    "uu": lambda u, v, z: (u + 2, v, z),
    "vv": lambda u, v, z: (u, v + 2, z),
}


def after(a, *others):
    return lax.optimization_barrier((a, others))[0]


BUFFERS = (
    ((2, 0), (2, 1), (3, 2), (3, 3)),
    ((2, 2), (2, 3), (1, 0), (1, 1)),
    ((3, 0), (3, 1), (1, 2), (1, 3)),
    ((0, 0), (0, 1), (0, 2), (0, 3)),
)


CHUNK = 64


def sort_kernel(act, cot, out, top, act_s, cot_s, out_s, in_sem, out_sem):
    u, v, z, turned = place()
    count = act.shape[0] // CHUNK
    for c in range(count):
        rows = pl.ds(c * CHUNK, CHUNK)
        pltpu.make_async_copy(act.at[rows], act_s.at[c], in_sem.at[0, c]).start()
        pltpu.make_async_copy(cot.at[rows], cot_s.at[c], in_sem.at[1, c]).start()

    def fold(value):
        m = None
        for i in range(value.shape[1] // 128):
            part = jnp.abs(value[:, i * 128 : (i + 1) * 128])
            m = part if m is None else jnp.maximum(m, part)
        return jnp.max(m.astype(F32).reshape(-1, 8, 128), axis=0)

    top[...] = jnp.zeros_like(top)

    @pl.loop(0, count)
    def _(c):
        pltpu.make_async_copy(act_s.at[c], act_s.at[c], in_sem.at[0, c]).wait()
        pltpu.make_async_copy(cot_s.at[c], cot_s.at[c], in_sem.at[1, c]).wait()
        for p in range(NZ):
            for b, slots in enumerate(BUFFERS):
                for k, (ju, jv) in enumerate(slots):
                    block = feature_block((u - ju) & 3, (v - jv) & 3, z ^ p, turned)
                    lanes = pl.ds(pl.multiple_of(block * 128, 128), 128)
                    out_s[c, p, b, :, k * 128 : (k + 1) * 128] = act_s[c, :, lanes]
        top[0] = jnp.maximum(top[0], fold(act_s[c]))
        top[1] = jnp.maximum(top[1], fold(cot_s[c]))
        rows = pl.ds(pl.multiple_of(c * CHUNK, CHUNK), CHUNK)
        pltpu.make_async_copy(out_s.at[c], out.at[:, :, rows], out_sem.at[c]).start()

    for c in range(count):
        pltpu.make_async_copy(out_s.at[c], out_s.at[c], out_sem.at[c]).wait()


def sort(act, cot):
    count = act.shape[0] // CHUNK
    any_ = pl.BlockSpec(memory_space=pl.ANY)
    return pl.pallas_call(
        sort_kernel,
        in_specs=[any_, any_],
        out_specs=[any_, pl.BlockSpec(memory_space=pltpu.VMEM)],
        out_shape=[
            jax.ShapeDtypeStruct((NZ, NX, act.shape[0], 512), BF16),
            jax.ShapeDtypeStruct((2, 8, 128), F32),
        ],
        scratch_shapes=[
            pltpu.VMEM((count, CHUNK, act.shape[1]), BF16),
            pltpu.VMEM((count, CHUNK, cot.shape[1]), BF16),
            pltpu.VMEM((count, NZ, NX, CHUNK, 512), BF16),
            pltpu.SemaphoreType.DMA((2, count)),
            pltpu.SemaphoreType.DMA((count,)),
        ],
        compiler_params=pltpu.CompilerParams(vmem_limit_bytes=56 << 20),
        cost_estimate=pl.CostEstimate(flops=0, bytes_accessed=1 << 20, transcendentals=0),
    )(act, cot)


def product_kernel(counts, before, *refs):
    act, cot = refs[0], refs[1]
    n = 2 + sum(counts.values())
    pieces = list(refs[2:n])
    partial = refs[n] if before else None
    n += 2 if before else 0
    proj, grad = refs[n], refs[n + 1]
    act_s, cot_s, w_s, acc_s, grad_s, a_sem, w_sem, c_sem, o_sem, p_sem = refs[n + 2 :]
    u, v, z, turned = place()

    def columns(p, ju, jv):
        block = feature_block((u - ju) & 3, (v - jv) & 3, z ^ p, turned)
        return pl.ds(pl.multiple_of(block * 128, 128), 128)

    cot_in = pltpu.make_async_copy(cot, cot_s, c_sem)
    cot_in.start()
    if before:
        sums_in = pltpu.make_async_copy(partial, acc_s, p_sem)
        sums_in.start()
    units = []
    for j, count in counts.items():
        halves = []
        for _ in range(count):
            part = pieces.pop(0)
            halves += [(part, begin) for begin in (0, LOW) if begin < part.shape[0]]
        units += [(p, j, [(part, begin + p * 256) for part, begin in halves]) for p in range(NZ)]
    for k, (p, j, halves) in enumerate(units):
        for h, (part, begin) in enumerate(halves):
            to = w_s.at[k, pl.ds(h * 256, 256)]
            pltpu.make_async_copy(part.at[pl.ds(begin, 256)], to, w_sem.at[k]).start()
        for i in range(NX):
            to = act_s.at[k, :, pl.ds(i * 128, 128)]
            pltpu.make_async_copy(act.at[:, columns(p, i, j)], to, a_sem.at[k]).start()
    cot_in.wait()
    if before:
        sums_in.wait()
    for k, (p, j, _) in enumerate(units):
        pltpu.make_async_copy(w_s.at[k], w_s.at[k], w_sem.at[k]).wait()
        pltpu.make_async_copy(act_s.at[k], act_s.at[k], a_sem.at[k]).wait()
        w = w_s[k]
        term = jnp.dot(act_s[k], w, preferred_element_type=F32)
        if k == 0 and not before:
            acc_s[...] = term
        else:
            acc_s[...] += term
        grad_s[k] = lax.dot_general(
            cot_s[...], w, (((1,), (1,)), ((), ())), preferred_element_type=F32
        ).astype(BF16)
        for i in range(NX):
            out = grad_s.at[k, :, pl.ds(i * 128, 128)]
            pltpu.make_async_copy(out, grad.at[:, columns(p, i, j)], o_sem.at[k]).start()
    proj[...] = acc_s[...].astype(proj.dtype)
    for k in range(len(units)):
        pltpu.make_async_copy(grad_s.at[k], grad_s.at[k], o_sem.at[k]).wait()


def products(act, cot, pieces, before=(), last=False):
    tokens, depth = act.shape
    width = cot.shape[1]
    counts = {j: len(parts) for j, parts in pieces.items()}
    flat = [part for parts in pieces.values() for part in parts]
    n = NZ * len(pieces)
    any_ = pl.BlockSpec(memory_space=pl.ANY)
    args = [act, cot, *flat, *before]
    return pl.pallas_call(
        lambda *refs: product_kernel(counts, bool(before), *refs),
        in_specs=[any_] * len(args),
        out_specs=[pl.BlockSpec(memory_space=pltpu.VMEM), any_],
        out_shape=[
            jax.ShapeDtypeStruct((tokens, width), BF16 if last else F32),
            jax.ShapeDtypeStruct((tokens, depth), BF16),
        ],
        input_output_aliases={len(args) - 1: 1} if before else {},
        scratch_shapes=[
            pltpu.VMEM((n, tokens, 512), BF16),
            pltpu.VMEM((tokens, width), BF16),
            pltpu.VMEM((n, 512, width), BF16),
            pltpu.VMEM((tokens, width), F32),
            pltpu.VMEM((n, tokens, 512), BF16),
            pltpu.SemaphoreType.DMA((n,)),
            pltpu.SemaphoreType.DMA((n,)),
            pltpu.SemaphoreType.DMA,
            pltpu.SemaphoreType.DMA((n,)),
            pltpu.SemaphoreType.DMA,
        ],
        compiler_params=pltpu.CompilerParams(vmem_limit_bytes=(8 + 3 * n) << 20),
        cost_estimate=pl.CostEstimate(flops=0, bytes_accessed=1 << 20, transcendentals=0),
    )(*args)


class Lanes:
    def __init__(self):
        self.last = {}

    def queue(self, lane, a, shift):
        if lane in self.last:
            a = after(a, self.last[lane])
        r = shift(a)
        self.last[lane] = r
        return r

    def send(self, lane, a, step=None):
        return self.queue(lane, a, lambda a: move(a, STEPS[step or lane]))

    def both(self, axis, forward, backward, lane=""):
        up, down = axis + "+", axis + "-"
        pair = self.send(lane + up, forward, up), self.send(lane + down, backward, down)
        return lax.optimization_barrier(pair)


def gather_v(lanes, a):
    f, b = lanes.both("v", a, a)
    low, high = lanes.both("v", f[:LOW], b[LOW:])
    return [a, f, low, high, b]


def join_kernel(cuts, *refs):
    arrays, out, sem = refs[:-2], refs[-2], refs[-1]
    copies = []
    for k, (which, begin, rows) in enumerate(cuts):
        from_ = arrays[which].at[pl.ds(begin, rows)]
        copies.append(pltpu.make_async_copy(from_, out.at[pl.ds(k * rows, rows)], sem.at[k]))
    for copy in copies:
        copy.start()
    for copy in copies:
        copy.wait()


def join(arrays, cuts):
    width = arrays[0].shape[1]
    total = sum(rows for _, _, rows in cuts)
    any_ = pl.BlockSpec(memory_space=pl.ANY)
    return pl.pallas_call(
        lambda *refs: join_kernel(cuts, *refs),
        in_specs=[any_] * len(arrays),
        out_specs=any_,
        out_shape=jax.ShapeDtypeStruct((total, width), arrays[0].dtype),
        scratch_shapes=[pltpu.SemaphoreType.DMA((len(cuts),))],
        compiler_params=pltpu.CompilerParams(vmem_limit_bytes=1 << 20),
        cost_estimate=pl.CostEstimate(flops=0, bytes_accessed=1 << 20, transcendentals=0),
    )(*arrays)


def gather_u(lanes, near, far, note):
    n = near.shape[0]
    own = jnp.concatenate([near, note], axis=0)
    f, o, b = all_of_ring(lanes, "u", own, own, own)
    far = after(far, f, o, b)
    far_f, far_o, far_b = all_of_ring(lanes, "u", far, far, far, "far ")
    row = join((near, f, far, far_f, o, b, far_o, far_b), [(m, 0, n) for m in range(2 * NX)])
    notes = [x[n:, :128].astype(F32) for x in (own, f, o, b)]
    return row, jnp.maximum(jnp.maximum(notes[0], notes[1]), jnp.maximum(notes[2], notes[3]))


def all_of_ring(lanes, axis, up, far, down, lane=""):
    f, b = lanes.both(axis, up, down, lane)
    return f, lanes.send(lane + "e", far, 2 * axis), b


def wide(*parts):
    total = parts[0].astype(F32)
    for p in parts[1:]:
        total = total + p.astype(F32)
    return total


def first_sums(buffers, arrived):
    half = buffers[0].shape[0] // 2
    f, b = arrived
    up = wide(buffers[2][:half], f[:half]).astype(F16)
    down = wide(buffers[2][half:], b[:half]).astype(F16)
    return up, down


def last_sums(buffers, arrived, sums):
    half = buffers[0].shape[0] // 2
    f, b = arrived
    f2, b2 = sums
    low = wide(buffers[3][:half], b[half:], f2)
    high = wide(buffers[3][half:], f[half:], b2)
    return [part.astype(F16) for part in (low, high)]


def with_note(a, exponent):
    note = jnp.broadcast_to(exponent.astype(F16), (NOTE, a.shape[1]))
    return jnp.concatenate([a, note], axis=0)


def exponent_in(a):
    return a[-NOTE : 1 - NOTE].astype(F32)


def reduce_v(lanes, low, high, exponent, behind, lane=""):
    n = low.shape[0] // 2
    low, high = after((low, high), *behind)
    sent = [with_note(part, exponent) for part in (high[n:], high[:n], low[n:])]
    got = all_of_ring(lanes, "v", *sent, lane)
    exponents = [exponent_in(part) for part in got]
    least = exponent
    for e in exponents:
        least = jnp.minimum(least, e)
    total = low[:n].astype(F32) * jnp.exp2(least - exponent)
    for part, e in zip(got, exponents):
        total = total + part[:-NOTE].astype(F32) * jnp.exp2(least - e)
    return total, least


def terms(act_sorted, cot, scale):
    out = []
    for part in act_sorted:
        g = jnp.einsum("td,tk->dk", part, cot, preferred_element_type=F32)
        out.append((g * scale).astype(F16))
    return out


def sum_of_replicas(lanes, codes, scale, phases):
    total = codes.astype(F32) * scale
    for bit in (1, 2, 4):
        pairs = [(j, j ^ bit) for j in range(NR)]
        if bit > 1:
            total = after(total, phases[bit // 2 - 1])
        total = total + lanes.queue("r", total, lambda a: lax.ppermute(a, "rep", pairs))
    return total


def exponent_for(note, tokens):
    bound = note[0, 0] * note[NOTE // 2, 0] * tokens
    return jnp.floor(jnp.log2(32768.0 / jnp.maximum(bound, 1e-30)))


def outer_step(average, params_rows, moment_rows):
    moment_next = 0.9 * moment_rows + average
    params_next = params_rows - 0.7 * (average + 0.9 * moment_next)
    return params_next, moment_next


def local(activations, weights, cotangent, quant_codes, replica_scale, outer_params, momentum):
    tokens = activations.shape[0] * lax.axis_size("fsdp")
    lanes = Lanes()
    shard = weights[0]
    far_shard = lanes.send("z", shard)
    act_sorted, top = sort(activations, cotangent)
    note = jnp.broadcast_to(jnp.max(top, axis=(1, 2))[:, None, None], (2, NOTE // 2, shard.shape[1]))
    row, note = gather_u(lanes, shard, far_shard, note.reshape(NOTE, -1).astype(BF16))
    exponent = exponent_for(note, tokens)
    scale = after(jnp.exp2(exponent), row)
    theirs = terms(act_sorted[1][:2], cotangent, scale)
    own, below, far_low, far_high, above = gather_v(lanes, row)
    theirs_in = lanes.both("u", theirs[0], theirs[1])
    phases = (far_shard, row)
    average = sum_of_replicas(lanes, quant_codes[0], replica_scale[0], phases) / lax.axis_size("rep")
    ready = after(cotangent, theirs, average)
    part = products(activations, ready, {0: [own]})
    theirs += terms(act_sorted[1][2:], ready, scale)
    mine = terms(act_sorted[0], cotangent, after(scale, theirs_in))

    sums = after(first_sums(theirs, theirs_in), below, above, part)
    theirs = last_sums(theirs, theirs_in, lanes.both("u", *sums))
    mine_in = lanes.both("u", *after((mine[0], mine[1]), far_low, far_high))
    theirs, their_exponent = reduce_v(lanes, *theirs, exponent, (), "theirs ")
    theirs = with_note(theirs.astype(F16), their_exponent)
    part = products(activations, after(cotangent, theirs), {1: [below], 3: [above]}, part)

    sums = after(first_sums(mine, mine_in), theirs, part)
    theirs = lanes.send("z", theirs)
    projected, input_grad = products(activations, after(cotangent, sums), {2: [far_low, far_high]}, part, last=True)
    mine = last_sums(mine, mine_in, lanes.both("u", *sums))
    mine, my_exponent = reduce_v(lanes, *mine, exponent, (projected, input_grad))
    total = mine * jnp.exp2(-my_exponent) + theirs[:-NOTE].astype(F32) * jnp.exp2(-exponent_in(theirs))
    gradient = total * (1.0 / jnp.sqrt(jnp.float32(tokens)))

    new_params, new_momentum = outer_step(average, outer_params, momentum)
    return projected, input_grad, gradient[None], new_params, new_momentum


def solution(mesh):
    placed = (
        P(("rep", "fsdp"), None),
        P("rep", "fsdp", None),
        P(("rep", "fsdp"), None),
        P("rep", "fsdp", None),
        P("rep"),
        P("fsdp", None),
        P("fsdp", None),
    )
    return jax.shard_map(
        local,
        mesh=mesh,
        in_specs=placed,
        out_specs=(
            P(("rep", "fsdp"), None),
            P(("rep", "fsdp"), None),
            P("rep", "fsdp", None),
            P("fsdp", None),
            P("fsdp", None),
        ),
        check_vma=False,
    )
```
